32 devices in a mesh: seq: 8 (over z, core), head: 4 (over y, x).
Axes of the slice: x: 2, y: 2, z: 4, core: 2. Of those that a mesh axis runs over, the one named last changes fastest.
Arguments:
- query_rows: bfloat16 [5120, 8192], P(('seq', 'head')), may hold values from -6 to 6
- rotated_key_rows: bfloat16 [5120, 1024], P(('seq', 'head')), may hold values from -6 to 6
- value_row_matrix: bfloat16 [5120, 1024], P(('seq', 'head')), may hold values from -6 to 6
- group_assign: int32 [64], replicated, may hold values from 0 to 63, each once
- vertical_blocks: int32 [64, 4], replicated, may hold values from 0 to 39
- slash_offsets: int32 [64, 3], replicated, may hold values from 0 to 5, as said below
Outputs:
- attended: bfloat16 [5120, 8192], P(('seq', 'head'))
The draws below stay inside these ranges and needn't reach their ends.
Inputs may be any that keep to these rules, and one draw needn't show every extreme that they name: `slash_offsets`: each head's first offset is 0 and its offsets are distinct.
All inputs are finite; a program needn't handle non-finite values.
Results may differ from the reference program's by a relative error of at most 0.0045.
Values may be sent and summed in bfloat16 or wider, within the bound.
A program may use at most 64 MiB of HBM per device.

```python
import math
import jax
import jax.numpy as jnp
from jax import lax

QUERY_HEADS = 64
KEY_VALUE_HEADS = 8
HEAD_SIZE = 128
BLOCK_TOKENS = 128
NV = 4
NS = 3
S_LOC = 640
SEQUENCE_TOKENS = 5120
NB = 40


def draw_query_rows(key, part):
    base_offset = jax.random.truncated_normal(jax.random.fold_in(key, 5), -6.0, 6.0, (SEQUENCE_TOKENS, QUERY_HEADS, HEAD_SIZE))
    return base_offset.reshape(SEQUENCE_TOKENS, QUERY_HEADS * HEAD_SIZE).astype(jnp.float32).astype(jnp.bfloat16)


def draw_rotated_key_rows(key, part):
    base_offset = jax.random.truncated_normal(jax.random.fold_in(key, 29), -6.0, 6.0, (SEQUENCE_TOKENS, KEY_VALUE_HEADS, HEAD_SIZE))
    return base_offset.reshape(SEQUENCE_TOKENS, KEY_VALUE_HEADS * HEAD_SIZE).astype(jnp.float32).astype(jnp.bfloat16)


def draw_slash_offsets(key, part):
    head_keys = jax.random.split(key, QUERY_HEADS)
    orders = jax.vmap(lambda single: jax.random.permutation(single, S_LOC // BLOCK_TOKENS))(head_keys) + 1
    leading = jnp.zeros((QUERY_HEADS, 1), jnp.int32)
    return jnp.concatenate([leading, orders[:, :NS - 1].astype(jnp.int32)], axis=1)


def set_ends(values, own_key, low, high):
    dims = values.shape
    spot = [jax.random.randint(jax.random.fold_in(own_key, axis), (), 0, dims[axis]) for axis in range(len(dims))]
    values = values.at[tuple(spot)].set(low)
    longest = dims.index(max(dims))
    spot[longest] = (spot[longest] + 1) % dims[longest]
    return values.at[tuple(spot)].set(high)


def shard_levels(own_key, extent, cuts, least, largest):
    def one(dim, parts):
        heights = jax.random.uniform(jax.random.fold_in(jax.random.fold_in(own_key, 6), dim), (parts,), jnp.float32, least / len(cuts), largest / len(cuts))
        return jnp.repeat(jnp.exp(heights), extent[dim] // parts).reshape((-1,) + (1,) * (len(extent) - dim - 1))

    factor_of = one(*cuts[0])
    for cut in cuts[1:]:
        factor_of = factor_of * one(*cut)
    return factor_of


def normal_values(rng, extent, spread, bound, cuts=(), kind=jnp.bfloat16):
    values = spread * jax.random.normal(rng, extent, jnp.float32)
    if cuts:
        values = values * shard_levels(rng, extent, cuts, -0.22, 0.18)
    return jnp.clip(values, -bound, bound).astype(kind)


def setup_inputs(seed: int = 0) -> dict:
    seeds = jax.random.split(jax.random.key(seed), 7)
    return {
        "query_rows": draw_query_rows(jax.random.fold_in(seeds[6], 71), 0),
        "rotated_key_rows": draw_rotated_key_rows(jax.random.fold_in(seeds[6], 71), 0),
        "value_row_matrix": normal_values(seeds[2], (SEQUENCE_TOKENS, KEY_VALUE_HEADS * HEAD_SIZE), 1.0, 6.0, ((0, 32),)),
        "group_assign": jax.random.permutation(seeds[3], QUERY_HEADS).astype(jnp.int32),
        "vertical_blocks": set_ends(jax.random.randint(seeds[4], (QUERY_HEADS, NV), 0, NB), jax.random.fold_in(seeds[4], 1), 0, NB - 1).astype(jnp.int32),
        "slash_offsets": draw_slash_offsets(jax.random.fold_in(seeds[6], 71), 0),
    }


def reference(query_rows, rotated_key_rows, value_row_matrix, group_assign, vertical_blocks, slash_offsets):
    count_of_blocks = SEQUENCE_TOKENS // BLOCK_TOKENS
    sharing_count = QUERY_HEADS // KEY_VALUE_HEADS
    query_blocks = query_rows.reshape(count_of_blocks, BLOCK_TOKENS, QUERY_HEADS, HEAD_SIZE)
    blocked_keys = rotated_key_rows.reshape(count_of_blocks, BLOCK_TOKENS, KEY_VALUE_HEADS, HEAD_SIZE)
    blocked_values = value_row_matrix.reshape(count_of_blocks, BLOCK_TOKENS, KEY_VALUE_HEADS, HEAD_SIZE)
    block_ids = jnp.arange(count_of_blocks, dtype=jnp.int32)
    within = jnp.arange(BLOCK_TOKENS, dtype=jnp.int32)
    earlier = jnp.arange(NV)[:, None] < jnp.arange(NV)[None, :]
    scaling = 1.0 / math.sqrt(HEAD_SIZE)
    width_count = NS + NV

    def attend_head(head):
        kv_head = head // sharing_count
        queries_head = lax.dynamic_index_in_dim(query_blocks, head, 2, keepdims=False)
        keys_head = lax.dynamic_index_in_dim(blocked_keys, kv_head, 2, keepdims=False)
        values_head = lax.dynamic_index_in_dim(blocked_values, kv_head, 2, keepdims=False)
        offsets = slash_offsets[head]
        verticals = vertical_blocks[head]
        slash_cand = block_ids[:, None] - offsets[None, :]
        slash_ok = slash_cand >= 0
        repeated = jnp.any((verticals[:, None] == verticals[None, :]) & earlier, axis=0)
        covered = jnp.any(block_ids[:, None, None] - verticals[None, :, None] == offsets[None, None, :], axis=2)
        vert_ok = (verticals[None, :] <= block_ids[:, None]) & jnp.logical_not(covered) & jnp.logical_not(repeated)[None, :]
        candidates = jnp.concatenate([jnp.maximum(slash_cand, 0), jnp.broadcast_to(verticals[None, :], (count_of_blocks, NV))], axis=1).astype(jnp.int32)
        cand_ok = jnp.concatenate([slash_ok, vert_ok], axis=1)
        gathered_keys = keys_head[candidates].reshape(count_of_blocks, width_count * BLOCK_TOKENS, HEAD_SIZE)
        gathered_values = values_head[candidates].reshape(count_of_blocks, width_count * BLOCK_TOKENS, HEAD_SIZE)
        key_pos = (candidates[:, :, None] * BLOCK_TOKENS + within[None, None, :]).reshape(count_of_blocks, width_count * BLOCK_TOKENS)
        query_pos = block_ids[:, None] * BLOCK_TOKENS + within[None, :]
        allowed = jnp.repeat(cand_ok, BLOCK_TOKENS, axis=1)[:, None, :] & (key_pos[:, None, :] <= query_pos[:, :, None])
        scores = jnp.einsum('nqd,nkd->nqk', queries_head.astype(jnp.float32), gathered_keys.astype(jnp.float32)) * scaling
        row_top = lax.optimization_barrier(jnp.max(jnp.where(allowed, scores, -jnp.inf), axis=2, keepdims=True))
        weights = jnp.where(allowed, jnp.exp(scores - row_top), 0.0)
        row_total = lax.optimization_barrier(jnp.sum(weights, axis=2, keepdims=True))
        rounded = lax.optimization_barrier(weights.astype(jnp.bfloat16))
        blended = jnp.einsum('nqk,nkd->nqd', rounded.astype(jnp.float32), gathered_values.astype(jnp.float32)) / row_total
        return blended.astype(jnp.bfloat16)
    per_slot = lax.map(attend_head, group_assign)
    return jnp.transpose(per_slot, (1, 2, 0, 3)).reshape(SEQUENCE_TOKENS, QUERY_HEADS * HEAD_SIZE)
```

```python
import functools
import math

import jax
import jax.numpy as jnp
from jax import lax
from jax.experimental import pallas as pl
from jax.experimental.pallas import tpu as pltpu
from jax.sharding import PartitionSpec as P

QUERY_HEADS = 64
KEY_VALUE_HEADS = 8
HEAD_SIZE = 128
BLOCK_TOKENS = 128
SHARING = QUERY_HEADS // KEY_VALUE_HEADS
VMEM_BYTES = 56 * 1024 * 1024


def block_attention(query, keys_ref, values_ref, block, offsets, verticals):
    factor = math.log2(math.e) / math.sqrt(HEAD_SIZE)
    blocks, valid = [], []
    for offset in offsets:
        blocks.append(jnp.maximum(block - offset, 0))
        valid.append(block - offset >= 0)
    for n, vertical in enumerate(verticals):
        ok = vertical <= block
        for offset in offsets:
            ok = ok & (block - vertical != offset)
        for other in verticals[:n]:
            ok = ok & (vertical != other)
        blocks.append(jnp.minimum(vertical, block))
        valid.append(ok)
    places = [pl.ds(pl.multiple_of(b * BLOCK_TOKENS, BLOCK_TOKENS), BLOCK_TOKENS) for b in blocks]
    keys = jnp.concatenate([keys_ref[place, :] for place in places], axis=0)
    scores = lax.dot_general(
        query, keys, (((1,), (1,)), ((), ())), preferred_element_type=jnp.float32
    )
    parts = []
    for n in range(len(places)):
        part = scores[:, n * BLOCK_TOKENS : (n + 1) * BLOCK_TOKENS]
        if n == 0:
            rows = lax.broadcasted_iota(jnp.int32, part.shape, 0)
            columns = lax.broadcasted_iota(jnp.int32, part.shape, 1)
            part = jnp.where(columns <= rows, part, -jnp.inf)
        else:
            part = part + jnp.where(valid[n], 0.0, -jnp.inf)
        parts.append(part)
    top = functools.reduce(jnp.maximum, parts)
    row_top = jnp.max(top, axis=1, keepdims=True)
    weights = [jnp.exp2((part - row_top) * factor) for part in parts]
    row_total = jnp.sum(functools.reduce(jnp.add, weights), axis=1, keepdims=True)
    rounded = jnp.concatenate([w.astype(jnp.bfloat16) for w in weights], axis=1)
    values = jnp.concatenate([values_ref[place, :] for place in places], axis=0)
    blended = jnp.dot(rounded, values, preferred_element_type=jnp.float32)
    return (blended / row_total).astype(jnp.bfloat16)


def attention_kernel(share, nv, ns, place_ref, vert_ref, slash_ref, q_ref, k_ref, v_ref, o_ref):
    local_blocks = q_ref.shape[0] // BLOCK_TOKENS
    head = place_ref[1] + pl.program_id(0) * share + pl.program_id(1)
    offsets = [slash_ref[head * ns + n] for n in range(ns)]
    verticals = [vert_ref[head * nv + n] for n in range(nv)]
    for n in range(local_blocks):
        rows = pl.ds(n * BLOCK_TOKENS, BLOCK_TOKENS)
        block = place_ref[0] * local_blocks + n
        o_ref[rows, :] = block_attention(
            q_ref[rows, :], k_ref, v_ref, block, offsets, verticals
        )


def attend(query, keys_values, place, vertical_blocks, slash_offsets, kv_count):
    rows, width = query.shape
    heads = width // HEAD_SIZE
    share = heads // kv_count
    tokens = keys_values.shape[0]
    nv, ns = vertical_blocks.shape[1], slash_offsets.shape[1]
    pairs = heads * (rows // BLOCK_TOKENS) * (nv + ns)
    return pl.pallas_call(
        functools.partial(attention_kernel, share, nv, ns),
        grid_spec=pltpu.PrefetchScalarGridSpec(
            num_scalar_prefetch=3,
            grid=(kv_count, share),
            in_specs=[
                pl.BlockSpec((rows, HEAD_SIZE), lambda i, j, *_: (0, i * share + j)),
                pl.BlockSpec((tokens, HEAD_SIZE), lambda i, j, *_: (0, i)),
                pl.BlockSpec((tokens, HEAD_SIZE), lambda i, j, *_: (0, kv_count + i)),
            ],
            out_specs=pl.BlockSpec((rows, HEAD_SIZE), lambda i, j, *_: (0, i * share + j)),
        ),
        out_shape=jax.ShapeDtypeStruct(query.shape, query.dtype),
        compiler_params=pltpu.CompilerParams(vmem_limit_bytes=VMEM_BYTES),
        cost_estimate=pl.CostEstimate(
            flops=pairs * 4 * BLOCK_TOKENS * BLOCK_TOKENS * HEAD_SIZE,
            bytes_accessed=2 * query.nbytes + keys_values.nbytes,
            transcendentals=pairs * BLOCK_TOKENS * BLOCK_TOKENS,
        ),
    )(place, vertical_blocks.reshape(-1), slash_offsets.reshape(-1), query, keys_values, keys_values)


def reorder_kernel(per_step, assign_ref, x_ref, o_ref):
    step = pl.program_id(0)
    for n in range(per_step):
        source = assign_ref[step * per_step + n]
        column = pl.ds(pl.multiple_of(source * HEAD_SIZE, HEAD_SIZE), HEAD_SIZE)
        o_ref[:, n * HEAD_SIZE : (n + 1) * HEAD_SIZE] = x_ref[:, column]


def reorder(x, assign):
    per_step = 8
    rows, width = x.shape
    return pl.pallas_call(
        functools.partial(reorder_kernel, per_step),
        grid_spec=pltpu.PrefetchScalarGridSpec(
            num_scalar_prefetch=1,
            grid=(width // HEAD_SIZE // per_step,),
            in_specs=[pl.BlockSpec((rows, width), lambda i, *_: (0, 0))],
            out_specs=pl.BlockSpec((rows, per_step * HEAD_SIZE), lambda i, *_: (0, i)),
        ),
        out_shape=jax.ShapeDtypeStruct(x.shape, x.dtype),
        compiler_params=pltpu.CompilerParams(vmem_limit_bytes=VMEM_BYTES),
        cost_estimate=pl.CostEstimate(flops=0, bytes_accessed=2 * x.nbytes, transcendentals=0),
    )(assign, x)


def per_device(
    query_rows, rotated_key_rows, value_row_matrix, group_assign, vertical_blocks, slash_offsets
):
    groups = lax.axis_size("head")
    heads = QUERY_HEADS // groups
    kv_count = max(1, heads // SHARING)
    kv_width = kv_count * HEAD_SIZE
    pieces = []
    for g in range(groups):
        first = g * heads // SHARING * HEAD_SIZE
        pieces.append(rotated_key_rows[:, first : first + kv_width])
        pieces.append(value_row_matrix[:, first : first + kv_width])
    keys_values = jnp.concatenate(pieces, axis=1)
    keys_values = lax.all_to_all(keys_values, "head", split_axis=1, concat_axis=0, tiled=True)
    query_here = lax.all_to_all(query_rows, "head", split_axis=1, concat_axis=0, tiled=True)
    all_keys_values = lax.all_gather(keys_values, "seq", axis=0, tiled=True)
    place = jnp.stack([lax.axis_index("seq"), lax.axis_index("head") * heads]).astype(jnp.int32)
    attended = attend(
        query_here, all_keys_values, place, vertical_blocks, slash_offsets, kv_count
    )
    returned = lax.all_to_all(attended, "head", split_axis=0, concat_axis=1, tiled=True)
    return reorder(returned, group_assign)


def solution(mesh):
    placed = (
        P(("seq", "head"), None),
        P(("seq", "head"), None),
        P(("seq", "head"), None),
        P(),
        P(),
        P(),
    )
    return jax.shard_map(
        per_device, mesh=mesh, in_specs=placed, out_specs=P(("seq", "head"), None), check_vma=False
    )
```

```python
import functools
import math

import jax
import jax.numpy as jnp
from jax import lax
from jax.experimental import pallas as pl
from jax.experimental.pallas import tpu as pltpu
from jax.sharding import PartitionSpec as P

QUERY_HEADS = 64
KEY_VALUE_HEADS = 8
HEAD_SIZE = 128
BLOCK_TOKENS = 128
SHARING = QUERY_HEADS // KEY_VALUE_HEADS
VMEM_BYTES = 56 * 1024 * 1024


def block_attention(query, keys_values, key_column, value_column, block, offsets, verticals):
    factor = math.log2(math.e) / math.sqrt(HEAD_SIZE)
    blocks, valid = [], []
    for offset in offsets:
        blocks.append(jnp.maximum(block - offset, 0))
        valid.append(block - offset >= 0)
    for n, vertical in enumerate(verticals):
        ok = vertical <= block
        for offset in offsets:
            ok = ok & (block - vertical != offset)
        for other in verticals[:n]:
            ok = ok & (vertical != other)
        blocks.append(jnp.minimum(vertical, block))
        valid.append(ok)
    per_block = BLOCK_TOKENS // keys_values.shape[1]
    shape = (BLOCK_TOKENS, HEAD_SIZE)

    def gathered(column):
        return jnp.concatenate(
            [
                keys_values[pl.ds(b * per_block, per_block), :, column : column + HEAD_SIZE].reshape(shape)
                for b in blocks
            ],
            axis=0,
        )

    keys = gathered(key_column)
    scores = lax.dot_general(
        query, keys, (((1,), (1,)), ((), ())), preferred_element_type=jnp.float32
    )
    parts = []
    for n in range(len(blocks)):
        part = scores[:, n * BLOCK_TOKENS : (n + 1) * BLOCK_TOKENS]
        if n == 0:
            rows = lax.broadcasted_iota(jnp.int32, part.shape, 0)
            columns = lax.broadcasted_iota(jnp.int32, part.shape, 1)
            part = jnp.where(columns <= rows, part, -jnp.inf)
        else:
            part = part + jnp.where(valid[n], 0.0, -jnp.inf)
        parts.append(part)
    top = functools.reduce(jnp.maximum, parts)
    row_top = jnp.max(top, axis=1, keepdims=True)
    weights = [jnp.exp2((part - row_top) * factor) for part in parts]
    row_total = jnp.sum(functools.reduce(jnp.add, weights), axis=1, keepdims=True)
    rounded = jnp.concatenate([w.astype(jnp.bfloat16) for w in weights], axis=1)
    values = gathered(value_column)
    blended = jnp.dot(rounded, values, preferred_element_type=jnp.float32)
    return (blended / row_total).astype(jnp.bfloat16)


MESH = pl.DeviceIdType.MESH


def columns_of(start, count):
    return pl.ds(pl.multiple_of(start * count, HEAD_SIZE), count)


def units_of(start, count):
    return pl.ds(start * count, count)


def fused_kernel(
    nv, ns, assign_ref, vert_ref, slash_ref, query_ref, key_ref, value_ref, out_ref,
    queries, keys_values, attended, received,
    kv_send, kv_recv, q_send, q_recv, o_send, o_recv, own_sem, mine_sem,
    up_send, up_recv, pair_send, pair_recv,
):
    groups, seq_count = lax.axis_size("head"), lax.axis_size("seq")
    group, seq = lax.axis_index("head"), lax.axis_index("seq")
    chips = seq_count // 2
    core = lax.rem(seq, 2)
    pair = seq + 1 - 2 * core
    resident, unit = query_ref.shape[:2]
    heads = QUERY_HEADS // groups
    width = heads * HEAD_SIZE
    kv_width = keys_values.shape[2] // 2
    kv_count = kv_width // HEAD_SIZE
    share = heads // kv_count
    seq_rows = resident * groups
    per_block = BLOCK_TOKENS // unit
    local_blocks = seq_rows // per_block
    above, below = seq + 2 < seq_count, seq >= 2

    barrier = pltpu.get_barrier_semaphore()
    for d in range(1, groups):
        pl.semaphore_signal(
            barrier, inc=1, device_id={"head": lax.rem(group + d, groups)}, device_id_type=MESH
        )
    pl.semaphore_signal(barrier, inc=1, device_id={"seq": pair}, device_id_type=MESH)

    @pl.when(above)
    def _():
        pl.semaphore_signal(barrier, inc=1, device_id={"seq": seq + 2}, device_id_type=MESH)

    @pl.when(below)
    def _():
        pl.semaphore_signal(barrier, inc=1, device_id={"seq": seq - 2}, device_id_type=MESH)

    pl.semaphore_wait(barrier, groups + above.astype(jnp.int32) + below.astype(jnp.int32))

    def kv_columns(g):
        first = lax.div(g * heads, SHARING) * HEAD_SIZE
        return pl.ds(pl.multiple_of(first, HEAD_SIZE), kv_width)

    def kv_rows(g):
        return pl.ds(seq * seq_rows + g * resident, resident)

    def kv_copy(d, part, target, owner):
        source = (key_ref, value_ref)[part]
        return pltpu.make_async_remote_copy(
            src_ref=source.at[:, :, kv_columns(target)],
            dst_ref=keys_values.at[kv_rows(owner), :, pl.ds(part * kv_width, kv_width)],
            send_sem=kv_send.at[d, part],
            recv_sem=kv_recv.at[d, part],
            device_id={"head": target},
            device_id_type=MESH,
        )

    def q_copy(d, target, owner):
        return pltpu.make_async_remote_copy(
            src_ref=query_ref.at[:, :, columns_of(target, width)],
            dst_ref=queries.at[units_of(owner, resident)],
            send_sem=q_send.at[d],
            recv_sem=q_recv.at[d],
            device_id={"head": target},
            device_id_type=MESH,
        )

    def o_copy(d, h, target, owner):
        return pltpu.make_async_remote_copy(
            src_ref=attended.at[h, units_of(target, resident)],
            dst_ref=received.at[owner * heads + h],
            send_sem=o_send.at[d, h],
            recv_sem=o_recv.at[d, h],
            device_id={"head": target},
            device_id_type=MESH,
        )

    def mine_copy(h):
        return pltpu.make_async_copy(
            attended.at[h, units_of(group, resident)],
            received.at[group * heads + h],
            mine_sem.at[h],
        )

    def block_rows(b):
        return keys_values.at[units_of(b, seq_rows)]

    def up_copy(k, block, target, sem):
        return pltpu.make_async_remote_copy(
            src_ref=block_rows(block),
            dst_ref=block_rows(block),
            send_sem=up_send.at[k],
            recv_sem=up_recv.at[sem],
            device_id={"seq": target},
            device_id_type=MESH,
        )

    def pair_copy(k, block):
        return pltpu.make_async_remote_copy(
            src_ref=block_rows(block),
            dst_ref=block_rows(block),
            send_sem=pair_send.at[k],
            recv_sem=pair_recv.at[k],
            device_id={"seq": pair},
            device_id_type=MESH,
        )

    def later(d):
        return lax.rem(group + d, groups)

    def before(d):
        return lax.rem(group + groups - d, groups)

    for d in range(1, groups):
        for part in range(2):
            kv_copy(d, part, later(d), group).start()
    own = [
        pltpu.make_async_copy(
            source.at[:, :, kv_columns(group)],
            keys_values.at[kv_rows(group), :, pl.ds(part * kv_width, kv_width)],
            own_sem.at[part],
        )
        for part, source in enumerate((key_ref, value_ref))
    ]
    own.append(
        pltpu.make_async_copy(
            query_ref.at[:, :, columns_of(group, width)],
            queries.at[units_of(group, resident)],
            own_sem.at[2],
        )
    )
    for copy in own:
        copy.start()
    for d in range(1, groups):
        q_copy(d, later(d), group).start()
    own[0].wait()
    own[1].wait()
    for d in range(1, groups):
        for part in range(2):
            kv_copy(d, part, group, before(d)).wait_recv()

    for k in range(chips):
        block = seq - 2 * k
        held = block >= 0

        if k:

            @pl.when(held)
            def _():
                up_copy(k, block, seq, k).wait_recv()

        @pl.when(held & above)
        def _():
            up_copy(k, block, seq + 2, k + 1).start()

        @pl.when((held & (core == 0)) if k == 0 else held)
        def _():
            pair_copy(k, block).start()

    for k in range(chips):
        arrives = (core == 1) if k == 0 else pair - 2 * k >= 0

        @pl.when(arrives)
        def _():
            pair_copy(k, pair - 2 * k).wait_recv()

    own[2].wait()
    for d in range(1, groups):
        q_copy(d, group, before(d)).wait_recv()

    for kv in range(kv_count):
        key_column = kv * HEAD_SIZE

        def one_head(j, carry):
            h = kv * share + j
            head = group * heads + h
            offsets = [slash_ref[head * ns + n] for n in range(ns)]
            verticals = [vert_ref[head * nv + n] for n in range(nv)]
            column = columns_of(h, HEAD_SIZE)
            for n in range(local_blocks):
                part = pl.ds(n * per_block, per_block)
                blended = block_attention(
                    queries[part, :, column].reshape(BLOCK_TOKENS, HEAD_SIZE),
                    keys_values,
                    key_column,
                    kv_width + key_column,
                    seq * local_blocks + n,
                    offsets,
                    verticals,
                )
                attended[h, part] = blended.reshape(per_block, unit, HEAD_SIZE)
            for d in range(1, groups):
                o_copy(d, h, later(d), group).start()
            mine_copy(h).start()
            return carry

        lax.fori_loop(0, share, one_head, 0)

    def land(h, carry):
        mine_copy(h).wait()
        for d in range(1, groups):
            o_copy(d, h, group, before(d)).wait_recv()
        return carry

    lax.fori_loop(0, heads, land, 0)

    for k in range(QUERY_HEADS):
        out_ref[:, :, k * HEAD_SIZE : (k + 1) * HEAD_SIZE] = received[assign_ref[k]]

    def sent(h, carry):
        for d in range(1, groups):
            o_copy(d, h, later(d), group).wait_send()
        return carry

    lax.fori_loop(0, heads, sent, 0)
    for d in range(1, groups):
        q_copy(d, later(d), group).wait_send()
        for part in range(2):
            kv_copy(d, part, later(d), group).wait_send()
    for k in range(chips):
        block = seq - 2 * k
        held = block >= 0

        @pl.when(held & above)
        def _():
            up_copy(k, block, seq + 2, k + 1).wait_send()

        @pl.when((held & (core == 0)) if k == 0 else held)
        def _():
            pair_copy(k, block).wait_send()


def per_device(
    query_rows, rotated_key_rows, value_row_matrix, group_assign, vertical_blocks, slash_offsets
):
    groups, seq_count = lax.axis_size("head"), lax.axis_size("seq")
    heads = QUERY_HEADS // groups
    kv_count = max(1, heads // SHARING)
    rows = query_rows.shape[0]
    seq_rows = rows * groups
    unit = math.gcd(rows, BLOCK_TOKENS)
    nv, ns = vertical_blocks.shape[1], slash_offsets.shape[1]
    chips = seq_count // 2
    pairs = heads * (seq_rows // BLOCK_TOKENS) * (nv + ns)
    dma = pltpu.SemaphoreType.DMA
    kind = query_rows.dtype

    def in_units(x):
        return x.reshape(rows // unit, unit, x.shape[1])

    attended = pl.pallas_call(
        functools.partial(fused_kernel, nv, ns),
        out_shape=jax.ShapeDtypeStruct((rows // unit, unit, query_rows.shape[1]), kind),
        in_specs=[pl.BlockSpec(memory_space=pltpu.SMEM)] * 3
        + [pl.BlockSpec(memory_space=pl.ANY)] * 3,
        out_specs=pl.BlockSpec(memory_space=pltpu.VMEM),
        scratch_shapes=[
            pltpu.VMEM((seq_rows // unit, unit, heads * HEAD_SIZE), kind),
            pltpu.VMEM((seq_rows * seq_count // unit, unit, 2 * kv_count * HEAD_SIZE), kind),
            pltpu.VMEM((heads, seq_rows // unit, unit, HEAD_SIZE), kind),
            pltpu.VMEM((QUERY_HEADS, rows // unit, unit, HEAD_SIZE), kind),
            dma((groups, 2)),
            dma((groups, 2)),
            dma((groups,)),
            dma((groups,)),
            dma((groups, heads)),
            dma((groups, heads)),
            dma((3,)),
            dma((heads,)),
            dma((chips,)),
            dma((chips + 1,)),
            dma((chips,)),
            dma((chips,)),
        ],
        compiler_params=pltpu.CompilerParams(
            collective_id=0, has_side_effects=True, vmem_limit_bytes=VMEM_BYTES
        ),
        cost_estimate=pl.CostEstimate(
            flops=pairs * 4 * BLOCK_TOKENS * BLOCK_TOKENS * HEAD_SIZE,
            bytes_accessed=2 * query_rows.nbytes + 2 * rotated_key_rows.nbytes,
            transcendentals=pairs * BLOCK_TOKENS * BLOCK_TOKENS,
        ),
    )(
        group_assign, vertical_blocks.reshape(-1), slash_offsets.reshape(-1),
        in_units(query_rows), in_units(rotated_key_rows), in_units(value_row_matrix),
    )
    return attended.reshape(query_rows.shape)


def solution(mesh):
    placed = (
        P(("seq", "head"), None),
        P(("seq", "head"), None),
        P(("seq", "head"), None),
        P(),
        P(),
        P(),
    )
    return jax.shard_map(
        per_device, mesh=mesh, in_specs=placed, out_specs=P(("seq", "head"), None), check_vma=False
    )
```

```python
import functools
import math

import jax
import jax.numpy as jnp
from jax import lax
from jax.experimental import pallas as pl
from jax.experimental.pallas import tpu as pltpu
from jax.sharding import PartitionSpec as P

QUERY_HEADS = 64
KEY_VALUE_HEADS = 8
HEAD_SIZE = 128
BLOCK_TOKENS = 128
SHARING = QUERY_HEADS // KEY_VALUE_HEADS
VMEM_BYTES = 56 * 1024 * 1024


def block_attention(query, keys_values, key_column, value_column, block, offsets, verticals):
    factor = math.log2(math.e) / math.sqrt(HEAD_SIZE)
    blocks, valid = [], []
    for offset in offsets:
        blocks.append(jnp.maximum(block - offset, 0))
        valid.append(block - offset >= 0)
    for n, vertical in enumerate(verticals):
        ok = vertical <= block
        for offset in offsets:
            ok = ok & (block - vertical != offset)
        for other in verticals[:n]:
            ok = ok & (vertical != other)
        blocks.append(jnp.minimum(vertical, block))
        valid.append(ok)
    per_block = BLOCK_TOKENS // keys_values.shape[1]
    shape = (BLOCK_TOKENS, HEAD_SIZE)

    def gathered(column):
        return jnp.concatenate(
            [
                keys_values[pl.ds(b * per_block, per_block), :, column : column + HEAD_SIZE].reshape(shape)
                for b in blocks
            ],
            axis=0,
        )

    keys = gathered(key_column)
    scores = lax.dot_general(
        query, keys, (((1,), (1,)), ((), ())), preferred_element_type=jnp.float32
    )
    parts = []
    for n in range(len(blocks)):
        part = scores[:, n * BLOCK_TOKENS : (n + 1) * BLOCK_TOKENS]
        if n == 0:
            rows = lax.broadcasted_iota(jnp.int32, part.shape, 0)
            columns = lax.broadcasted_iota(jnp.int32, part.shape, 1)
            part = jnp.where(columns <= rows, part, -jnp.inf)
        else:
            part = part + jnp.where(valid[n], 0.0, -jnp.inf)
        parts.append(part)
    top = functools.reduce(jnp.maximum, parts)
    row_top = jnp.max(top, axis=1, keepdims=True)
    weights = [jnp.exp2((part - row_top) * factor) for part in parts]
    row_total = jnp.sum(functools.reduce(jnp.add, weights), axis=1, keepdims=True)
    rounded = jnp.concatenate([w.astype(jnp.bfloat16) for w in weights], axis=1)
    values = gathered(value_column)
    blended = jnp.dot(rounded, values, preferred_element_type=jnp.float32)
    return (blended / row_total).astype(jnp.bfloat16)


MESH = pl.DeviceIdType.MESH


def columns_of(start, count):
    return pl.ds(pl.multiple_of(start * count, HEAD_SIZE), count)


def units_of(start, count):
    return pl.ds(start * count, count)


def fused_kernel(
    nv, ns, assign_ref, vert_ref, slash_ref, query_ref, key_ref, value_ref, out_ref,
    attended, received,
    kv_send, kv_recv, q_send, q_recv, o_send, o_recv, own_sem, mine_sem,
    up_send, up_recv, pair_send, pair_recv, *by_kv,
):
    groups, seq_count = lax.axis_size("head"), lax.axis_size("seq")
    group, seq = lax.axis_index("head"), lax.axis_index("seq")
    chips = seq_count // 2
    core = lax.rem(seq, 2)
    pair = seq + 1 - 2 * core
    resident, unit = query_ref.shape[:2]
    heads = QUERY_HEADS // groups
    kv_count = len(by_kv) // 2
    queries, keys_values = by_kv[:kv_count], by_kv[kv_count:]
    share = heads // kv_count
    width = share * HEAD_SIZE
    seq_rows = resident * groups
    per_block = BLOCK_TOKENS // unit
    local_blocks = seq_rows // per_block
    above, below = seq + 2 < seq_count, seq >= 2

    barrier = pltpu.get_barrier_semaphore()
    for d in range(1, groups):
        pl.semaphore_signal(
            barrier, inc=1, device_id={"head": lax.rem(group + d, groups)}, device_id_type=MESH
        )
    pl.semaphore_signal(barrier, inc=1, device_id={"seq": pair}, device_id_type=MESH)

    @pl.when(above)
    def _():
        pl.semaphore_signal(barrier, inc=1, device_id={"seq": seq + 2}, device_id_type=MESH)

    @pl.when(below)
    def _():
        pl.semaphore_signal(barrier, inc=1, device_id={"seq": seq - 2}, device_id_type=MESH)

    pl.semaphore_wait(barrier, groups + above.astype(jnp.int32) + below.astype(jnp.int32))

    def kv_columns(g, kv):
        return columns_of(lax.div(g * heads, SHARING) + kv, HEAD_SIZE)

    def half(part):
        return pl.ds(part * HEAD_SIZE, HEAD_SIZE)

    def kv_rows(g):
        return pl.ds(seq * seq_rows + g * resident, resident)

    def kv_copy(d, kv, part, target, owner):
        source = (key_ref, value_ref)[part]
        return pltpu.make_async_remote_copy(
            src_ref=source.at[:, :, kv_columns(target, kv)],
            dst_ref=keys_values[kv].at[kv_rows(owner), :, half(part)],
            send_sem=kv_send.at[d, kv, part],
            recv_sem=kv_recv.at[d, kv, part],
            device_id={"head": target},
            device_id_type=MESH,
        )

    def q_copy(d, kv, target, owner):
        return pltpu.make_async_remote_copy(
            src_ref=query_ref.at[:, :, columns_of(target * kv_count + kv, width)],
            dst_ref=queries[kv].at[units_of(owner, resident)],
            send_sem=q_send.at[d, kv],
            recv_sem=q_recv.at[d, kv],
            device_id={"head": target},
            device_id_type=MESH,
        )

    def o_copy(d, h, target, owner):
        return pltpu.make_async_remote_copy(
            src_ref=attended.at[h, units_of(target, resident)],
            dst_ref=received.at[owner * heads + h],
            send_sem=o_send.at[d, h],
            recv_sem=o_recv.at[d, h],
            device_id={"head": target},
            device_id_type=MESH,
        )

    def mine_copy(h):
        return pltpu.make_async_copy(
            attended.at[h, units_of(group, resident)],
            received.at[group * heads + h],
            mine_sem.at[h],
        )

    def block_rows(kv, b):
        return keys_values[kv].at[units_of(b, seq_rows)]

    def up_copy(kv, k, block, target, sem):
        return pltpu.make_async_remote_copy(
            src_ref=block_rows(kv, block),
            dst_ref=block_rows(kv, block),
            send_sem=up_send.at[kv, k],
            recv_sem=up_recv.at[kv, sem],
            device_id={"seq": target},
            device_id_type=MESH,
        )

    def pair_copy(kv, k, block):
        return pltpu.make_async_remote_copy(
            src_ref=block_rows(kv, block),
            dst_ref=block_rows(kv, block),
            send_sem=pair_send.at[kv, k],
            recv_sem=pair_recv.at[kv, k],
            device_id={"seq": pair},
            device_id_type=MESH,
        )

    def later(d):
        return lax.rem(group + d, groups)

    def before(d):
        return lax.rem(group + groups - d, groups)

    own_kv = [
        [
            pltpu.make_async_copy(
                source.at[:, :, kv_columns(group, kv)],
                keys_values[kv].at[kv_rows(group), :, half(part)],
                own_sem.at[kv, part],
            )
            for part, source in enumerate((key_ref, value_ref))
        ]
        for kv in range(kv_count)
    ]
    own_q = [
        pltpu.make_async_copy(
            query_ref.at[:, :, columns_of(group * kv_count + kv, width)],
            queries[kv].at[units_of(group, resident)],
            own_sem.at[kv, 2],
        )
        for kv in range(kv_count)
    ]

    def send_kv(kv):
        for d in range(1, groups):
            for part in range(2):
                kv_copy(d, kv, part, later(d), group).start()
        for copy in own_kv[kv]:
            copy.start()

    def await_kv(kv):
        for copy in own_kv[kv]:
            copy.wait()
        for d in range(1, groups):
            for part in range(2):
                kv_copy(d, kv, part, group, before(d)).wait_recv()

    def send_q(kv):
        for d in range(1, groups):
            q_copy(d, kv, later(d), group).start()
        own_q[kv].start()

    def chain_step(kv, k):
        block = seq - 2 * k
        held = block >= 0
        if k:

            @pl.when(held)
            def _():
                up_copy(kv, k, block, seq, k).wait_recv()

        @pl.when(held & above)
        def _():
            up_copy(kv, k, block, seq + 2, k + 1).start()

        @pl.when((held & (core == 0)) if k == 0 else held)
        def _():
            pair_copy(kv, k, block).start()

    send_kv(0)
    await_kv(0)
    chain_step(0, 0)
    for kv in range(1, kv_count):
        send_kv(kv)
    send_q(0)
    for k in range(1, chips):
        chain_step(0, k)
        if k == 1:
            for kv in range(1, kv_count):
                send_q(kv)

    for kv in range(kv_count):
        following = kv + 1
        if following < kv_count:
            await_kv(following)
            chain_step(following, 0)
        for k in range(chips):
            arrives = (core == 1) if k == 0 else pair - 2 * k >= 0

            @pl.when(arrives)
            def _():
                pair_copy(kv, k, pair - 2 * k).wait_recv()

        own_q[kv].wait()
        for d in range(1, groups):
            q_copy(d, kv, group, before(d)).wait_recv()

        def one_head(j, carry):
            h = kv * share + j
            head = group * heads + h
            offsets = [slash_ref[head * ns + n] for n in range(ns)]
            verticals = [vert_ref[head * nv + n] for n in range(nv)]
            column = columns_of(j, HEAD_SIZE)
            for n in range(local_blocks):
                part = pl.ds(n * per_block, per_block)
                blended = block_attention(
                    queries[kv][part, :, column].reshape(BLOCK_TOKENS, HEAD_SIZE),
                    keys_values[kv],
                    0,
                    HEAD_SIZE,
                    seq * local_blocks + n,
                    offsets,
                    verticals,
                )
                attended[h, part] = blended.reshape(per_block, unit, HEAD_SIZE)
            for d in range(1, groups):
                o_copy(d, h, later(d), group).start()
            mine_copy(h).start()
            if following < kv_count:
                for k in range(1, chips):

                    @pl.when(j == min(share, 2 + 2 * k) - 1)
                    def _():
                        chain_step(following, k)

            return carry

        lax.fori_loop(0, share, one_head, 0)

    def land(h, carry):
        mine_copy(h).wait()
        for d in range(1, groups):
            o_copy(d, h, group, before(d)).wait_recv()
        return carry

    lax.fori_loop(0, heads, land, 0)

    for k in range(QUERY_HEADS):
        out_ref[:, :, k * HEAD_SIZE : (k + 1) * HEAD_SIZE] = received[assign_ref[k]]

    def sent(h, carry):
        for d in range(1, groups):
            o_copy(d, h, later(d), group).wait_send()
        return carry

    lax.fori_loop(0, heads, sent, 0)
    for kv in range(kv_count):
        for d in range(1, groups):
            q_copy(d, kv, later(d), group).wait_send()
            for part in range(2):
                kv_copy(d, kv, part, later(d), group).wait_send()
        for k in range(chips):
            block = seq - 2 * k
            held = block >= 0

            @pl.when(held & above)
            def _():
                up_copy(kv, k, block, seq + 2, k + 1).wait_send()

            @pl.when((held & (core == 0)) if k == 0 else held)
            def _():
                pair_copy(kv, k, block).wait_send()


def per_device(
    query_rows, rotated_key_rows, value_row_matrix, group_assign, vertical_blocks, slash_offsets
):
    groups, seq_count = lax.axis_size("head"), lax.axis_size("seq")
    heads = QUERY_HEADS // groups
    kv_count = max(1, heads // SHARING)
    rows = query_rows.shape[0]
    seq_rows = rows * groups
    unit = math.gcd(rows, BLOCK_TOKENS)
    nv, ns = vertical_blocks.shape[1], slash_offsets.shape[1]
    chips = seq_count // 2
    pairs = heads * (seq_rows // BLOCK_TOKENS) * (nv + ns)
    dma = pltpu.SemaphoreType.DMA
    kind = query_rows.dtype

    def in_units(x):
        return x.reshape(rows // unit, unit, x.shape[1])

    attended = pl.pallas_call(
        functools.partial(fused_kernel, nv, ns),
        out_shape=jax.ShapeDtypeStruct((rows // unit, unit, query_rows.shape[1]), kind),
        in_specs=[pl.BlockSpec(memory_space=pltpu.SMEM)] * 3
        + [pl.BlockSpec(memory_space=pl.ANY)] * 3,
        out_specs=pl.BlockSpec(memory_space=pltpu.VMEM),
        scratch_shapes=[
            pltpu.VMEM((heads, seq_rows // unit, unit, HEAD_SIZE), kind),
            pltpu.VMEM((QUERY_HEADS, rows // unit, unit, HEAD_SIZE), kind),
            dma((groups, kv_count, 2)),
            dma((groups, kv_count, 2)),
            dma((groups, kv_count)),
            dma((groups, kv_count)),
            dma((groups, heads)),
            dma((groups, heads)),
            dma((kv_count, 3)),
            dma((heads,)),
            dma((kv_count, chips)),
            dma((kv_count, chips + 1)),
            dma((kv_count, chips)),
            dma((kv_count, chips)),
        ]
        + [pltpu.VMEM((seq_rows // unit, unit, heads // kv_count * HEAD_SIZE), kind)] * kv_count
        + [pltpu.VMEM((seq_rows * seq_count // unit, unit, 2 * HEAD_SIZE), kind)] * kv_count,
        compiler_params=pltpu.CompilerParams(
            collective_id=0, has_side_effects=True, vmem_limit_bytes=VMEM_BYTES
        ),
        cost_estimate=pl.CostEstimate(
            flops=pairs * 4 * BLOCK_TOKENS * BLOCK_TOKENS * HEAD_SIZE,
            bytes_accessed=2 * query_rows.nbytes + 2 * rotated_key_rows.nbytes,
            transcendentals=pairs * BLOCK_TOKENS * BLOCK_TOKENS,
        ),
    )(
        group_assign, vertical_blocks.reshape(-1), slash_offsets.reshape(-1),
        in_units(query_rows), in_units(rotated_key_rows), in_units(value_row_matrix),
    )
    return attended.reshape(query_rows.shape)


def solution(mesh):
    placed = (
        P(("seq", "head"), None),
        P(("seq", "head"), None),
        P(("seq", "head"), None),
        P(),
        P(),
        P(),
    )
    return jax.shard_map(
        per_device, mesh=mesh, in_specs=placed, out_specs=P(("seq", "head"), None), check_vma=False
    )
```
